32 devices in a mesh: angle: 4 (over x, core), gz: 8 (over z, y).
Axes of the slice: x: 2, y: 2, z: 4, core: 2. Of those that a mesh axis runs over, the one named last changes fastest.
Arguments:
- projections: bfloat16 [48, 128, 4096], P('angle', 'gz'), may hold values from -6 to 6
- partner_view: int32 [48], P('angle'), may hold values from 0 to 47, as said below
- row_weight: bfloat16 [48, 128], P('angle', 'gz'), may hold values from 0.099609375 to 1
- row_slab: int32 [48, 128], P('angle', 'gz'), may hold values from 0 to 127, as said below
Outputs:
- slab_sinogram: bfloat16 [48, 128, 8192], P('angle', 'gz')
The draws below stay inside these ranges and needn't reach their ends.
Inputs may be any that keep to these rules, and one draw needn't show every extreme that they name: `partner_view`: the partner of a view lies in the block of 12 views whose block index differs by half the number of blocks (2); the partner of the partner is the view itself. `row_slab`: owner of slab s is s // 16. Among the 12 x 16 rows of one device (one block of views and one block of detector rows), at most 48 go to the slabs of any one owner; in every draw, for each block of views, some owner receives exactly 48 rows from every block of detector rows.
All inputs are finite; a program needn't handle non-finite values.
Results may differ from the reference program's by a relative error of at most 0.001.
Values may be sent and summed in bfloat16 or wider, within the bound.
A program may use at most 128 MiB of HBM per device.

```python
import math
import jax
import jax.numpy as jnp
from jax import lax

CH = 4096
OV = 128
KB = 256
VB = 12
RB = 16
SLAB_DEV = 16
VIEWS = 48
ROWS = 128
NSLAB = 128
W = 8192


def draw_partner_view(key, part):
    key = jax.random.fold_in(key, 11)
    block_count = VIEWS // VB
    half_blocks = block_count // 2

    def per_block(block):
        shuffled = jax.random.permutation(jax.random.fold_in(key, block), VB)
        inverse = jnp.argsort(shuffled, stable=True)
        lower = (block + half_blocks) * VB + shuffled
        upper = block * VB + inverse
        return (lower, upper)
    lower, upper = jax.vmap(per_block)(jnp.arange(half_blocks))
    return jnp.concatenate([lower.reshape(-1), upper.reshape(-1)]).astype(jnp.int32)


def draw_row_slab(key, part):
    key = jax.random.fold_in(key, 23)
    angle_blocks = VIEWS // VB
    owner_count = ROWS // RB
    block_rows = VB * RB
    capacity = 2 * block_rows // owner_count
    remaining = block_rows - capacity
    hottest = jax.random.randint(jax.random.fold_in(key, 1), (angle_blocks,), 0, owner_count)
    block_base = jax.random.fold_in(key, 5)

    def per_block(angle_index, row_index):
        subkey = jax.random.fold_in(jax.random.fold_in(block_base, angle_index), row_index)
        key_weight, key_order, key_local = jax.random.split(subkey, 3)
        is_hot = jnp.arange(owner_count) == hottest[angle_index]
        shares = jnp.where(is_hot, 0, jax.random.randint(key_weight, (owner_count,), 1, 3))
        base = remaining * shares // jnp.sum(shares)
        leftover = remaining - jnp.sum(base)
        standing = jnp.cumsum(jnp.where(is_hot, 0, 1)) - 1
        extra = jnp.where(jnp.logical_and(jnp.logical_not(is_hot), standing < leftover), 1, 0)
        counts = jnp.where(is_hot, capacity, base + extra)
        ends = jnp.cumsum(counts)
        positions = jnp.arange(block_rows)
        sorted_owner = jnp.sum((positions[:, None] >= ends[None, :]).astype(jnp.int32), 1)
        owners = sorted_owner[jax.random.permutation(key_order, block_rows)]
        local_slab = jax.random.randint(key_local, (block_rows,), 0, SLAB_DEV)
        return (owners * SLAB_DEV + local_slab).reshape(VB, RB)
    blocks = jax.vmap(lambda angle_index: jax.vmap(lambda row_index: per_block(angle_index, row_index))(jnp.arange(owner_count)))(jnp.arange(angle_blocks))
    return blocks.transpose(0, 2, 1, 3).reshape(VIEWS, ROWS).astype(jnp.int32)


def level_of(key, dims, pieces, smallest, high):
    level = 1.0
    for axis_at, blocks in pieces:
        heights = jax.random.uniform(jax.random.fold_in(jax.random.fold_in(key, 6), axis_at), (blocks,), jnp.float32, smallest / len(pieces), high / len(pieces))
        level = level * jnp.repeat(jnp.exp(heights), dims[axis_at] // blocks).reshape((-1,) + (1,) * (len(dims) - 1 - axis_at))
    return level


def bell_draw(rng, shape, deviation, reach, cuts=(), held_as=jnp.bfloat16):
    gain = level_of(rng, shape, cuts, -0.22, 0.18) if cuts else 1.0
    values = jax.random.normal(rng, shape, jnp.float32) * deviation * gain
    return jnp.minimum(jnp.maximum(values, -reach), reach).astype(held_as)


def setup_inputs(seed: int = 0) -> dict:
    arg_keys = jax.random.split(jax.random.key(seed), 5)
    return {
        "projections": bell_draw(arg_keys[0], (VIEWS, ROWS, CH), 1.0, 6.0, ((0, 4), (1, 8))),
        "partner_view": draw_partner_view(jax.random.fold_in(arg_keys[4], 71), 0),
        "row_weight": jnp.clip(0.099609375 + 0.9003906 * jax.random.uniform(arg_keys[2], (VIEWS, ROWS), jnp.float32) ** level_of(arg_keys[2], (VIEWS, ROWS), ((0, 4), (1, 8)), -0.2, 0.2), 0.099609375, 1.0).astype(jnp.bfloat16),
        "row_slab": draw_row_slab(jax.random.fold_in(arg_keys[4], 71), 0),
    }


def kernel_taps(size, shift):
    column = jnp.arange(size)[:, None]
    outrow = jnp.arange(size)[None, :]
    offset = outrow - column + shift
    distance = offset.astype(jnp.float32)
    squared = jnp.maximum(distance * distance, 1.0)
    is_odd = (offset % 2) != 0
    values = jnp.where(offset == 0, 0.25, jnp.where(is_odd, -1.0 / (math.pi * math.pi * squared), 0.0))
    return jnp.where(jnp.abs(offset) <= size, values, 0.0).astype(jnp.float32)


def ramp_filter(rows, size):
    before = kernel_taps(size, size)
    middle = kernel_taps(size, 0)
    after = kernel_taps(size, -size)
    row_count, width = rows.shape
    blocks = rows.reshape(row_count, width // size, size)
    padded = jnp.pad(blocks, ((0, 0), (1, 1), (0, 0)))
    highest = lax.Precision.HIGHEST
    result = jnp.einsum("nbk,km->nbm", padded[:, :-2], before, precision=highest)
    result = result + jnp.einsum("nbk,km->nbm", padded[:, 1:-1], middle, precision=highest)
    result = result + jnp.einsum("nbk,km->nbm", padded[:, 2:], after, precision=highest)
    return result.reshape(row_count, width)


def stitch_rows(own_rows, mirror_rows):
    channels = own_rows.shape[-1]
    position = jnp.arange(2 * channels).astype(jnp.float32)
    ramp_part = jnp.clip((position - (channels - OV) + 0.5) / (2.0 * OV), 0.0, 1.0)
    feather = jnp.sin(0.5 * math.pi * ramp_part) ** 2
    leading_pad = [(0, 0)] * (own_rows.ndim - 1)
    own_placed = jnp.pad(own_rows.astype(jnp.float32), leading_pad + [(channels - OV, OV)])
    mirror_placed = jnp.pad(jnp.flip(mirror_rows, -1).astype(jnp.float32), leading_pad + [(OV, channels - OV)])
    return feather * own_placed + (1.0 - feather) * mirror_placed


def reference(projections, partner_view, row_weight, row_slab):
    mirrored = projections[partner_view]

    def per_view(inputs):
        own_rows, mirror_rows, weights, slabs = inputs
        stitched = stitch_rows(own_rows, mirror_rows)
        filtered = ramp_filter(stitched, KB)
        weighted = filtered * weights.astype(jnp.float32)[:, None]
        summed = jnp.zeros((NSLAB, W), jnp.float32).at[slabs.astype(jnp.int32)].add(weighted)
        return summed.astype(jnp.bfloat16)

    return lax.map(per_view, (projections, mirrored, row_weight, row_slab))
```

```python
import functools
import math

import jax
import jax.numpy as jnp
from jax import lax
from jax.experimental import pallas as pl
from jax.experimental.pallas import tpu as pltpu
from jax.sharding import PartitionSpec as P
import ml_dtypes
import numpy as np

OV = 128
KB = 256
SLAB_DEV = 16
CHUNKS = 2
BF = jnp.bfloat16
F32 = jnp.float32
MESH = pl.DeviceIdType.MESH


def taps(size):
    offset = np.arange(size)[None, :] + size - np.arange(3 * size)[:, None]
    squared = np.maximum(offset.astype(np.float64) ** 2, 1.0)
    values = np.where(
        offset == 0, 0.25, np.where(offset % 2 != 0, -1.0 / (math.pi * math.pi * squared), 0.0)
    )
    return np.where(np.abs(offset) <= size, values, 0.0).astype(np.float32)


def exchange_kernel(
    owners, blocks, chunk, raw_ref, pick_own_ref, pick_mirror_ref, flip_ref, got_ref,
    flipped, outgoing, send_sem, recv_sem, local_sem,
):
    me_a, me_g = lax.axis_index("angle"), lax.axis_index("gz")
    partner = lax.rem(me_a + blocks // 2, blocks)
    slots = outgoing.shape[3]
    channels = raw_ref.shape[1]
    barrier = pltpu.get_barrier_semaphore()
    for kind in range(2):
        target_a = me_a if kind == 0 else partner
        for step in range(1 - kind, owners):
            pl.semaphore_signal(
                barrier, inc=1, device_id=(target_a, lax.rem(me_g + step, owners)),
                device_id_type=MESH,
            )
    width = 2 * KB
    for at in range(channels // KB):
        block = jnp.dot(raw_ref[:, at * KB:(at + 1) * KB], flip_ref[...], preferred_element_type=F32)
        to = channels - (at + 1) * KB
        flipped[:, to:to + KB] = block.astype(BF)
    pl.semaphore_wait(barrier, 2 * owners - 1)
    copies = []
    for part in range(channels // chunk):
        for kind in range(2):
            pick = pick_own_ref if kind == 0 else pick_mirror_ref
            source = raw_ref if kind == 0 else flipped
            for at in range(chunk // width):
                begin = part * chunk + at * width
                rows = jnp.dot(pick[...], source[:, begin:begin + width], preferred_element_type=F32)
                rows = rows.astype(BF).reshape(owners, slots, width)
                outgoing[part, kind, :, :, at * width:(at + 1) * width] = rows
            target_a = me_a if kind == 0 else partner
            for step in range(owners - 1, -1, -1):
                to = lax.rem(me_g + step, owners)
                if kind == 0 and step == 0:
                    copy = pltpu.make_async_copy(
                        outgoing.at[part, kind, me_g], got_ref.at[part, kind, me_g],
                        local_sem.at[part],
                    )
                else:
                    copy = pltpu.make_async_remote_copy(
                        src_ref=outgoing.at[part, kind, to],
                        dst_ref=got_ref.at[part, kind, me_g],
                        send_sem=send_sem.at[part, kind, step],
                        recv_sem=recv_sem.at[part, kind, step],
                        device_id=(target_a, to),
                        device_id_type=MESH,
                    )
                copy.start()
                copies.append(copy)
    for copy in copies:
        copy.wait()


def exchange(raw, pick_own, pick_mirror, flip, owners, blocks, slots):
    rows, channels = raw.shape
    chunk = channels // CHUNKS
    vmem = pl.BlockSpec(memory_space=pltpu.VMEM)
    return pl.pallas_call(
        functools.partial(exchange_kernel, owners, blocks, chunk),
        out_shape=jax.ShapeDtypeStruct((CHUNKS, 2, owners, slots, chunk), BF),
        in_specs=[vmem] * 4,
        out_specs=pl.BlockSpec(memory_space=pl.ANY),
        scratch_shapes=[
            pltpu.VMEM((rows, channels), BF),
            pltpu.VMEM((CHUNKS, 2, owners, slots, chunk), BF),
            pltpu.SemaphoreType.DMA((CHUNKS, 2, owners)),
            pltpu.SemaphoreType.DMA((CHUNKS, 2, owners)),
            pltpu.SemaphoreType.DMA((CHUNKS,)),
        ],
        compiler_params=pltpu.CompilerParams(
            collective_id=0, has_side_effects=True, vmem_limit_bytes=48 * 2**20
        ),
        name="exchange",
    )(raw, pick_own, pick_mirror, flip)


def filter_kernel(got_ref, sum_ref, high_ref, low_ref, feather_ref, out_ref, high, low):
    parts, _, _, chunk = got_ref.shape
    channels = parts * chunk
    count = channels // KB
    pad = 2 * KB
    for ref in (high, low):
        ref[:, :pad] = jnp.zeros((ref.shape[0], pad), BF)
        ref[:, ref.shape[1] - pad:] = jnp.zeros((ref.shape[0], pad), BF)

    def summed(kind, at):
        part, begin = at * KB // chunk, at * KB % chunk
        return jnp.dot(
            sum_ref[...], got_ref[part, kind, :, begin:begin + KB], preferred_element_type=F32
        )

    for at in range(2 * count - 1):
        if at < count - 1:
            value = summed(1, at)
        elif at >= count:
            value = summed(0, at - count + 1)
        else:
            weight = feather_ref[...]
            value = weight * summed(0, 0) + (1.0 - weight) * summed(1, at)
        top = value.astype(BF)
        place = pl.ds(pad + at * KB, KB)
        high[:, place] = top
        low[:, place] = (value - top.astype(F32)).astype(BF)
    for at in range(-1, 2 * count):
        window = pl.ds(pad + (at - 1) * KB, 3 * KB)
        value = jnp.dot(high[:, window], high_ref[...], preferred_element_type=F32)
        value += jnp.dot(high[:, window], low_ref[...], preferred_element_type=F32)
        value += jnp.dot(low[:, window], high_ref[...], preferred_element_type=F32)
        value = value.astype(BF)
        begin = OV + at * KB
        if at < 0:
            out_ref[:, :OV] = value[:, OV:]
        elif at == 2 * count - 1:
            out_ref[:, begin:] = value[:, :OV]
        else:
            out_ref[:, begin:begin + KB] = value


def filtered_slabs(got, sums, feather):
    parts, kinds, owners, slots, chunk = got.shape
    channels = parts * chunk
    rows = sums.shape[0]
    tap = taps(KB)
    tap_high = tap.astype(ml_dtypes.bfloat16)
    tap_low = (tap - tap_high.astype(np.float32)).astype(ml_dtypes.bfloat16)
    vmem = pl.BlockSpec(memory_space=pltpu.VMEM)
    return pl.pallas_call(
        filter_kernel,
        out_shape=jax.ShapeDtypeStruct((rows, 2 * channels), BF),
        in_specs=[vmem] * 5,
        out_specs=vmem,
        scratch_shapes=[pltpu.VMEM((rows, 2 * channels - KB + 4 * KB), BF)] * 2,
        compiler_params=pltpu.CompilerParams(vmem_limit_bytes=56 * 2**20),
        name="filter",
    )(got.reshape(parts, kinds, owners * slots, chunk), sums, jnp.asarray(tap_high), jnp.asarray(tap_low), feather)


def ranked(owner, owners):
    rows = owner.shape[-1]
    onehot = (owner[..., None] == jnp.arange(owners)).astype(BF)
    earlier = (jnp.arange(rows)[:, None] > jnp.arange(rows)[None, :]).astype(BF)
    before = jnp.einsum("rk,...ko->...ro", earlier, onehot, preferred_element_type=F32)
    return jnp.sum(before * onehot.astype(F32), -1).astype(jnp.int32)


def local(projections, partner_view, row_weight, row_slab):
    blocks, owners = lax.axis_size("angle"), lax.axis_size("gz")
    views, rows_dev, channels = projections.shape
    rows = views * rows_dev
    capacity = 2 * rows // owners
    slots = -(-capacity // 16) * 16
    half = blocks // 2
    other_slab = lax.ppermute(row_slab, "angle", [(s, (s + half) % blocks) for s in range(blocks)])
    meta = lax.all_gather(
        jnp.concatenate([row_slab.astype(F32), row_weight.astype(F32)], 0), "gz", axis=0
    )

    def slot_of(slab):
        owner = slab.reshape(rows) // SLAB_DEV
        return owner * slots + ranked(owner, owners)

    own_slot = slot_of(row_slab)
    other_slot = slot_of(other_slab).reshape(views, rows_dev)
    local_partner = partner_view % views
    is_partner = (local_partner[:, None] == jnp.arange(views)[None, :]).astype(jnp.int32)
    mirror_slot = jnp.sum(is_partner[:, :, None] * other_slot[None], 1).reshape(rows)
    slot_list = jnp.arange(owners * slots)[:, None]
    pick_own = (own_slot[None, :] == slot_list).astype(BF)
    pick_mirror = (mirror_slot[None, :] == slot_list).astype(BF)
    flip = (jnp.arange(KB)[:, None] + jnp.arange(KB)[None, :] == KB - 1).astype(BF)
    got = exchange(
        projections.reshape(rows, channels), pick_own, pick_mirror, flip, owners, blocks, slots
    )

    all_slab = meta[:, :views].reshape(owners, rows).astype(jnp.int32)
    all_weight = meta[:, views:].reshape(owners, rows).astype(BF)
    owner = all_slab // SLAB_DEV
    slot = jnp.where(owner == lax.axis_index("gz"), ranked(owner, owners), -1)
    target = jnp.arange(rows) // rows_dev * SLAB_DEV + all_slab % SLAB_DEV
    goes = jnp.where(
        target[:, None, :] == jnp.arange(views * SLAB_DEV)[:, None], all_weight[:, None, :], 0
    ).astype(BF)
    stands = (slot[:, :, None] == jnp.arange(slots)).astype(BF)
    sums = jnp.einsum("gtr,grs->tgs", goes, stands, preferred_element_type=F32)
    sums = sums.astype(BF).reshape(views * SLAB_DEV, owners * slots)
    ramp_part = np.clip((np.arange(KB) + 0.5) / (2.0 * OV), 0.0, 1.0)
    feather = jnp.asarray((np.sin(0.5 * math.pi * ramp_part) ** 2)[None, :], F32)
    return filtered_slabs(got, sums, feather).reshape(views, SLAB_DEV, 2 * channels)


def solution(mesh):
    in_specs = (P("angle", "gz", None), P("angle"), P("angle", "gz"), P("angle", "gz"))
    out_specs = P("angle", "gz", None)
    return jax.shard_map(local, mesh=mesh, in_specs=in_specs, out_specs=out_specs, check_vma=False)
```

```python
import functools
import math

import jax
import jax.numpy as jnp
from jax import lax
from jax.experimental import pallas as pl
from jax.experimental.pallas import tpu as pltpu
from jax.sharding import PartitionSpec as P
import ml_dtypes
import numpy as np

OV = 128
KB = 256
SLAB_DEV = 16
CHUNKS = 2
BF = jnp.bfloat16
F32 = jnp.float32
MESH = pl.DeviceIdType.MESH


def taps(size):
    offset = np.arange(size)[None, :] + size - np.arange(3 * size)[:, None]
    squared = np.maximum(offset.astype(np.float64) ** 2, 1.0)
    values = np.where(
        offset == 0, 0.25, np.where(offset % 2 != 0, -1.0 / (math.pi * math.pi * squared), 0.0)
    )
    return np.where(np.abs(offset) <= size, values, 0.0).astype(np.float32)


def exchange_kernel(
    owners, blocks, chunk, raw_ref, pick_own_ref, pick_mirror_ref, flip_ref, lists_ref, got_ref,
    got_lists_ref, flipped, outgoing, send_sem, recv_sem, local_sem, lists_send, lists_recv,
):
    me_a, me_g = lax.axis_index("angle"), lax.axis_index("gz")
    partner = lax.rem(me_a + blocks // 2, blocks)
    slots = outgoing.shape[3]
    channels = raw_ref.shape[1]
    barrier = pltpu.get_barrier_semaphore()
    for kind in range(2):
        target_a = me_a if kind == 0 else partner
        for step in range(1 - kind, owners):
            pl.semaphore_signal(
                barrier, inc=1, device_id=(target_a, lax.rem(me_g + step, owners)),
                device_id_type=MESH,
            )
    width = 2 * KB
    for at in range(channels // KB):
        block = jnp.dot(raw_ref[:, at * KB:(at + 1) * KB], flip_ref[...], preferred_element_type=F32)
        to = channels - (at + 1) * KB
        flipped[:, to:to + KB] = block.astype(BF)
    pl.semaphore_wait(barrier, 2 * owners - 1)
    copies = []
    for step in range(owners):
        if step == 0:
            copy = pltpu.make_async_copy(lists_ref, got_lists_ref.at[me_g], lists_send.at[0])
        else:
            copy = pltpu.make_async_remote_copy(
                src_ref=lists_ref,
                dst_ref=got_lists_ref.at[me_g],
                send_sem=lists_send.at[step],
                recv_sem=lists_recv.at[step],
                device_id=(me_a, lax.rem(me_g + step, owners)),
                device_id_type=MESH,
            )
        copy.start()
        copies.append(copy)
    for part in range(channels // chunk):
        for kind in range(2):
            pick = pick_own_ref if kind == 0 else pick_mirror_ref
            source = raw_ref if kind == 0 else flipped
            for at in range(chunk // width):
                begin = part * chunk + at * width
                rows = jnp.dot(pick[...], source[:, begin:begin + width], preferred_element_type=F32)
                rows = rows.astype(BF).reshape(owners, slots, width)
                outgoing[part, kind, :, :, at * width:(at + 1) * width] = rows
            target_a = me_a if kind == 0 else partner
            for step in range(owners - 1, -1, -1):
                to = lax.rem(me_g + step, owners)
                if kind == 0 and step == 0:
                    copy = pltpu.make_async_copy(
                        outgoing.at[part, kind, me_g], got_ref.at[part, kind, me_g],
                        local_sem.at[part],
                    )
                else:
                    copy = pltpu.make_async_remote_copy(
                        src_ref=outgoing.at[part, kind, to],
                        dst_ref=got_ref.at[part, kind, me_g],
                        send_sem=send_sem.at[part, kind, step],
                        recv_sem=recv_sem.at[part, kind, step],
                        device_id=(target_a, to),
                        device_id_type=MESH,
                    )
                copy.start()
                copies.append(copy)
    for copy in copies:
        copy.wait()


def exchange(raw, pick_own, pick_mirror, flip, lists, owners, blocks, slots):
    rows, channels = raw.shape
    chunk = channels // CHUNKS
    vmem = pl.BlockSpec(memory_space=pltpu.VMEM)
    return pl.pallas_call(
        functools.partial(exchange_kernel, owners, blocks, chunk),
        out_shape=[
            jax.ShapeDtypeStruct((CHUNKS, 2, owners, slots, chunk), BF),
            jax.ShapeDtypeStruct((owners,) + lists.shape, F32),
        ],
        in_specs=[vmem] * 5,
        out_specs=[pl.BlockSpec(memory_space=pl.ANY)] * 2,
        scratch_shapes=[
            pltpu.VMEM((rows, channels), BF),
            pltpu.VMEM((CHUNKS, 2, owners, slots, chunk), BF),
            pltpu.SemaphoreType.DMA((CHUNKS, 2, owners)),
            pltpu.SemaphoreType.DMA((CHUNKS, 2, owners)),
            pltpu.SemaphoreType.DMA((CHUNKS,)),
            pltpu.SemaphoreType.DMA((owners,)),
            pltpu.SemaphoreType.DMA((owners,)),
        ],
        compiler_params=pltpu.CompilerParams(
            collective_id=0, has_side_effects=True, vmem_limit_bytes=48 * 2**20
        ),
        name="exchange",
    )(raw, pick_own, pick_mirror, flip, lists)


def filter_kernel(got_ref, sum_ref, high_ref, low_ref, feather_ref, out_ref, high, low):
    parts, _, _, chunk = got_ref.shape
    channels = parts * chunk
    count = channels // KB
    pad = 2 * KB
    for ref in (high, low):
        ref[:, :pad] = jnp.zeros((ref.shape[0], pad), BF)
        ref[:, ref.shape[1] - pad:] = jnp.zeros((ref.shape[0], pad), BF)

    def summed(kind, at):
        part, begin = at * KB // chunk, at * KB % chunk
        return jnp.dot(
            sum_ref[...], got_ref[part, kind, :, begin:begin + KB], preferred_element_type=F32
        )

    for at in range(2 * count - 1):
        if at < count - 1:
            value = summed(1, at)
        elif at >= count:
            value = summed(0, at - count + 1)
        else:
            weight = feather_ref[...]
            value = weight * summed(0, 0) + (1.0 - weight) * summed(1, at)
        top = value.astype(BF)
        place = pl.ds(pad + at * KB, KB)
        high[:, place] = top
        low[:, place] = (value - top.astype(F32)).astype(BF)
    for at in range(-1, 2 * count):
        window = pl.ds(pad + (at - 1) * KB, 3 * KB)
        value = jnp.dot(high[:, window], high_ref[...], preferred_element_type=F32)
        value += jnp.dot(high[:, window], low_ref[...], preferred_element_type=F32)
        value += jnp.dot(low[:, window], high_ref[...], preferred_element_type=F32)
        value = value.astype(BF)
        begin = OV + at * KB
        if at < 0:
            out_ref[:, :OV] = value[:, OV:]
        elif at == 2 * count - 1:
            out_ref[:, begin:] = value[:, :OV]
        else:
            out_ref[:, begin:begin + KB] = value


def filtered_slabs(got, sums, feather):
    parts, kinds, owners, slots, chunk = got.shape
    channels = parts * chunk
    rows = sums.shape[0]
    tap = taps(KB)
    tap_high = tap.astype(ml_dtypes.bfloat16)
    tap_low = (tap - tap_high.astype(np.float32)).astype(ml_dtypes.bfloat16)
    vmem = pl.BlockSpec(memory_space=pltpu.VMEM)
    return pl.pallas_call(
        filter_kernel,
        out_shape=jax.ShapeDtypeStruct((rows, 2 * channels), BF),
        in_specs=[vmem] * 5,
        out_specs=vmem,
        scratch_shapes=[pltpu.VMEM((rows, 2 * channels - KB + 4 * KB), BF)] * 2,
        compiler_params=pltpu.CompilerParams(vmem_limit_bytes=56 * 2**20),
        name="filter",
    )(got.reshape(parts, kinds, owners * slots, chunk), sums, jnp.asarray(tap_high), jnp.asarray(tap_low), feather)


def ranked(owner, owners):
    rows = owner.shape[-1]
    onehot = (owner[..., None] == jnp.arange(owners)).astype(BF)
    earlier = (jnp.arange(rows)[:, None] > jnp.arange(rows)[None, :]).astype(BF)
    before = jnp.einsum("rk,...ko->...ro", earlier, onehot, preferred_element_type=F32)
    return jnp.sum(before * onehot.astype(F32), -1).astype(jnp.int32)


def local(projections, partner_view, row_weight, row_slab):
    blocks, owners = lax.axis_size("angle"), lax.axis_size("gz")
    views, rows_dev, channels = projections.shape
    rows = views * rows_dev
    capacity = 2 * rows // owners
    slots = -(-capacity // 16) * 16
    half = blocks // 2
    other_slab = lax.ppermute(row_slab, "angle", [(s, (s + half) % blocks) for s in range(blocks)])
    lists = jnp.concatenate([row_slab.astype(F32), row_weight.astype(F32)], 0)
    lists = jnp.pad(lists, ((0, 0), (0, 128 - rows_dev)))

    def slot_of(slab):
        owner = slab.reshape(rows) // SLAB_DEV
        return owner * slots + ranked(owner, owners)

    own_slot = slot_of(row_slab)
    other_slot = slot_of(other_slab).reshape(views, rows_dev)
    local_partner = partner_view % views
    is_partner = (local_partner[:, None] == jnp.arange(views)[None, :]).astype(jnp.int32)
    mirror_slot = jnp.sum(is_partner[:, :, None] * other_slot[None], 1).reshape(rows)
    slot_list = jnp.arange(owners * slots)[:, None]
    pick_own = (own_slot[None, :] == slot_list).astype(BF)
    pick_mirror = (mirror_slot[None, :] == slot_list).astype(BF)
    flip = (jnp.arange(KB)[:, None] + jnp.arange(KB)[None, :] == KB - 1).astype(BF)
    got, meta = exchange(
        projections.reshape(rows, channels), pick_own, pick_mirror, flip, lists, owners, blocks,
        slots,
    )
    meta = meta[:, :, :rows_dev]

    all_slab = meta[:, :views].reshape(owners, rows).astype(jnp.int32)
    all_weight = meta[:, views:].reshape(owners, rows).astype(BF)
    owner = all_slab // SLAB_DEV
    slot = jnp.where(owner == lax.axis_index("gz"), ranked(owner, owners), -1)
    target = jnp.arange(rows) // rows_dev * SLAB_DEV + all_slab % SLAB_DEV
    goes = jnp.where(
        target[:, None, :] == jnp.arange(views * SLAB_DEV)[:, None], all_weight[:, None, :], 0
    ).astype(BF)
    stands = (slot[:, :, None] == jnp.arange(slots)).astype(BF)
    sums = jnp.einsum("gtr,grs->tgs", goes, stands, preferred_element_type=F32)
    sums = sums.astype(BF).reshape(views * SLAB_DEV, owners * slots)
    ramp_part = np.clip((np.arange(KB) + 0.5) / (2.0 * OV), 0.0, 1.0)
    feather = jnp.asarray((np.sin(0.5 * math.pi * ramp_part) ** 2)[None, :], F32)
    return filtered_slabs(got, sums, feather).reshape(views, SLAB_DEV, 2 * channels)


def solution(mesh):
    in_specs = (P("angle", "gz", None), P("angle"), P("angle", "gz"), P("angle", "gz"))
    out_specs = P("angle", "gz", None)
    return jax.shard_map(local, mesh=mesh, in_specs=in_specs, out_specs=out_specs, check_vma=False)
```

```python
import functools
import math

import jax
import jax.numpy as jnp
from jax import lax
from jax.experimental import pallas as pl
from jax.experimental.pallas import tpu as pltpu
from jax.sharding import PartitionSpec as P
import ml_dtypes
import numpy as np

OV = 128
KB = 256
SLAB_DEV = 16
CHUNKS = 4
BF = jnp.bfloat16
F32 = jnp.float32
MESH = pl.DeviceIdType.MESH


def taps(size):
    offset = np.arange(size)[None, :] + size - np.arange(3 * size)[:, None]
    squared = np.maximum(offset.astype(np.float64) ** 2, 1.0)
    values = np.where(
        offset == 0, 0.25, np.where(offset % 2 != 0, -1.0 / (math.pi * math.pi * squared), 0.0)
    )
    return np.where(np.abs(offset) <= size, values, 0.0).astype(np.float32)


def exchange_kernel(
    owners, blocks, chunk, raw_ref, pick_ref, flip_ref, lists_ref, got_ref, got_lists_ref, far,
    flipped, outgoing, send_sem, recv_sem, local_sem, far_send, far_recv, lists_send, lists_recv,
):
    me_a, me_g = lax.axis_index("angle"), lax.axis_index("gz")
    partner = lax.rem(me_a + blocks // 2, blocks)
    half = owners // 2
    base = me_g // half * half
    place = me_g - base
    far_g = lax.rem(me_g + half, owners)
    slots = outgoing.shape[4]
    parts = raw_ref.shape[1] // chunk
    barrier = pltpu.get_barrier_semaphore()
    for step in range(1, owners):
        pl.semaphore_signal(
            barrier, inc=1, device_id=(me_a, lax.rem(me_g + step, owners)), device_id_type=MESH
        )
    for step in range(half):
        pl.semaphore_signal(
            barrier, inc=1, device_id=(partner, base + lax.rem(place + step, half)),
            device_id_type=MESH,
        )
    pl.semaphore_wait(barrier, owners - 1 + half)
    copies, crossing = [], []
    for part in range(parts):
        copy = pltpu.make_async_remote_copy(
            src_ref=raw_ref.at[:, part * chunk:(part + 1) * chunk],
            dst_ref=far.at[part],
            send_sem=far_send.at[part],
            recv_sem=far_recv.at[part],
            device_id=(me_a, far_g),
            device_id_type=MESH,
        )
        copy.start()
        crossing.append(copy)
    for step in range(owners):
        if step == 0:
            copy = pltpu.make_async_copy(lists_ref, got_lists_ref.at[me_g], lists_send.at[0])
        else:
            copy = pltpu.make_async_remote_copy(
                src_ref=lists_ref,
                dst_ref=got_lists_ref.at[me_g],
                send_sem=lists_send.at[step],
                recv_sem=lists_recv.at[step],
                device_id=(me_a, lax.rem(me_g + step, owners)),
                device_id_type=MESH,
            )
        copy.start()
        copies.append(copy)
    width = 2 * KB
    for origin in range(2):
        source_g = me_g if origin == 0 else far_g
        for part in range(parts):
            if origin == 1:
                crossing[part].wait()
            for at in range(chunk // KB):
                begin = part * chunk + at * KB
                block = (
                    raw_ref[:, begin:begin + KB] if origin == 0
                    else far[part, :, at * KB:(at + 1) * KB]
                )
                block = jnp.dot(block, flip_ref[...], preferred_element_type=F32)
                to = chunk - (at + 1) * KB
                flipped[:, to:to + KB] = block.astype(BF)
            for kind in range(2):
                out_part = part if kind == 0 else parts - 1 - part
                for at in range(0, chunk, width):
                    if kind == 1:
                        block = flipped[:, at:at + width]
                    elif origin == 0:
                        block = raw_ref[:, part * chunk + at:part * chunk + at + width]
                    else:
                        block = far[part, :, at:at + width]
                    rows = jnp.dot(pick_ref[origin, kind], block, preferred_element_type=F32)
                    outgoing[out_part, kind, origin, :, :, at:at + width] = (
                        rows.astype(BF).reshape(half, slots, width)
                    )
                target_a = me_a if kind == 0 else partner
                for step in range(half - 1, -1, -1):
                    to = lax.rem(place + step, half)
                    source = outgoing.at[out_part, kind, origin, to]
                    target = got_ref.at[out_part, kind, source_g]
                    if kind == 0 and step == 0:
                        copy = pltpu.make_async_copy(source, target, local_sem.at[part, origin])
                    else:
                        copy = pltpu.make_async_remote_copy(
                            src_ref=source,
                            dst_ref=target,
                            send_sem=send_sem.at[out_part, kind, origin, step],
                            recv_sem=recv_sem.at[out_part, kind, origin, step],
                            device_id=(target_a, base + to),
                            device_id_type=MESH,
                        )
                    copy.start()
                    copies.append(copy)
    for copy in copies:
        copy.wait()


def exchange(raw, pick, flip, lists, owners, blocks, slots):
    rows, channels = raw.shape
    chunk = channels // CHUNKS
    vmem = pl.BlockSpec(memory_space=pltpu.VMEM)
    return pl.pallas_call(
        functools.partial(exchange_kernel, owners, blocks, chunk),
        out_shape=[
            jax.ShapeDtypeStruct((CHUNKS, 2, owners, slots, chunk), BF),
            jax.ShapeDtypeStruct((owners,) + lists.shape, F32),
        ],
        in_specs=[vmem] * 4,
        out_specs=[pl.BlockSpec(memory_space=pl.ANY)] * 2,
        scratch_shapes=[
            pltpu.VMEM((CHUNKS, rows, chunk), BF),
            pltpu.VMEM((rows, chunk), BF),
            pltpu.VMEM((CHUNKS, 2, 2, owners // 2, slots, chunk), BF),
            pltpu.SemaphoreType.DMA((CHUNKS, 2, 2, owners // 2)),
            pltpu.SemaphoreType.DMA((CHUNKS, 2, 2, owners // 2)),
            pltpu.SemaphoreType.DMA((CHUNKS, 2)),
            pltpu.SemaphoreType.DMA((CHUNKS,)),
            pltpu.SemaphoreType.DMA((CHUNKS,)),
            pltpu.SemaphoreType.DMA((owners,)),
            pltpu.SemaphoreType.DMA((owners,)),
        ],
        compiler_params=pltpu.CompilerParams(
            collective_id=0, has_side_effects=True, vmem_limit_bytes=48 * 2**20
        ),
        name="exchange",
    )(raw, pick, flip, lists)


def filter_kernel(got_ref, sum_ref, high_ref, low_ref, feather_ref, out_ref, high, low):
    parts, _, _, chunk = got_ref.shape
    channels = parts * chunk
    count = channels // KB
    pad = 2 * KB
    for ref in (high, low):
        ref[:, :pad] = jnp.zeros((ref.shape[0], pad), BF)
        ref[:, ref.shape[1] - pad:] = jnp.zeros((ref.shape[0], pad), BF)

    def summed(kind, at):
        part, begin = at * KB // chunk, at * KB % chunk
        return jnp.dot(
            sum_ref[...], got_ref[part, kind, :, begin:begin + KB], preferred_element_type=F32
        )

    for at in range(2 * count - 1):
        if at < count - 1:
            value = summed(1, at)
        elif at >= count:
            value = summed(0, at - count + 1)
        else:
            weight = feather_ref[...]
            value = weight * summed(0, 0) + (1.0 - weight) * summed(1, at)
        top = value.astype(BF)
        place = pl.ds(pad + at * KB, KB)
        high[:, place] = top
        low[:, place] = (value - top.astype(F32)).astype(BF)
    for at in range(-1, 2 * count):
        window = pl.ds(pad + (at - 1) * KB, 3 * KB)
        value = jnp.dot(high[:, window], high_ref[...], preferred_element_type=F32)
        value += jnp.dot(high[:, window], low_ref[...], preferred_element_type=F32)
        value += jnp.dot(low[:, window], high_ref[...], preferred_element_type=F32)
        value = value.astype(BF)
        begin = OV + at * KB
        if at < 0:
            out_ref[:, :OV] = value[:, OV:]
        elif at == 2 * count - 1:
            out_ref[:, begin:] = value[:, :OV]
        else:
            out_ref[:, begin:begin + KB] = value


def filtered_slabs(got, sums, feather):
    parts, kinds, owners, slots, chunk = got.shape
    channels = parts * chunk
    rows = sums.shape[0]
    tap = taps(KB)
    tap_high = tap.astype(ml_dtypes.bfloat16)
    tap_low = (tap - tap_high.astype(np.float32)).astype(ml_dtypes.bfloat16)
    vmem = pl.BlockSpec(memory_space=pltpu.VMEM)
    return pl.pallas_call(
        filter_kernel,
        out_shape=jax.ShapeDtypeStruct((rows, 2 * channels), BF),
        in_specs=[vmem] * 5,
        out_specs=vmem,
        scratch_shapes=[pltpu.VMEM((rows, 2 * channels - KB + 4 * KB), BF)] * 2,
        compiler_params=pltpu.CompilerParams(vmem_limit_bytes=56 * 2**20),
        name="filter",
    )(got.reshape(parts, kinds, owners * slots, chunk), sums, jnp.asarray(tap_high), jnp.asarray(tap_low), feather)


def ranked(owner, owners):
    rows = owner.shape[-1]
    onehot = (owner[..., None] == jnp.arange(owners)).astype(BF)
    earlier = (jnp.arange(rows)[:, None] > jnp.arange(rows)[None, :]).astype(BF)
    before = jnp.einsum("rk,...ko->...ro", earlier, onehot, preferred_element_type=F32)
    return jnp.sum(before * onehot.astype(F32), -1).astype(jnp.int32)


def local(projections, partner_view, row_weight, row_slab):
    blocks, owners = lax.axis_size("angle"), lax.axis_size("gz")
    views, rows_dev, channels = projections.shape
    rows = views * rows_dev
    capacity = 2 * rows // owners
    slots = -(-capacity // 16) * 16
    half = blocks // 2
    other_slab = lax.ppermute(row_slab, "angle", [(s, (s + half) % blocks) for s in range(blocks)])
    lists = jnp.concatenate([row_slab.astype(F32), row_weight.astype(F32)], 0)
    lists = jnp.pad(lists, ((0, 0), (0, 128 - rows_dev)))

    def slot_of(slab):
        owner = slab.reshape(rows) // SLAB_DEV
        return owner * slots + ranked(owner, owners)

    pair = jnp.stack([row_slab, other_slab])
    far = owners // 2
    far_pair = lax.ppermute(pair, "gz", [(s, (s + far) % owners) for s in range(owners)])
    local_partner = partner_view % views
    is_partner = (local_partner[:, None] == jnp.arange(views)[None, :]).astype(jnp.int32)
    slot_list = (lax.axis_index("gz") // far * far * slots + jnp.arange(far * slots))[:, None]

    def picks(own_slab, partner_slab):
        own_slot = slot_of(own_slab)
        other_slot = slot_of(partner_slab).reshape(views, rows_dev)
        mirror_slot = jnp.sum(is_partner[:, :, None] * other_slot[None], 1).reshape(rows)
        return jnp.stack([own_slot[None, :] == slot_list, mirror_slot[None, :] == slot_list])

    pick = jnp.stack([picks(pair[0], pair[1]), picks(far_pair[0], far_pair[1])]).astype(BF)
    flip = (jnp.arange(KB)[:, None] + jnp.arange(KB)[None, :] == KB - 1).astype(BF)
    got, meta = exchange(
        projections.reshape(rows, channels), pick, flip, lists, owners, blocks, slots
    )
    meta = meta[:, :, :rows_dev]

    all_slab = meta[:, :views].reshape(owners, rows).astype(jnp.int32)
    all_weight = meta[:, views:].reshape(owners, rows).astype(BF)
    owner = all_slab // SLAB_DEV
    slot = jnp.where(owner == lax.axis_index("gz"), ranked(owner, owners), -1)
    target = jnp.arange(rows) // rows_dev * SLAB_DEV + all_slab % SLAB_DEV
    goes = jnp.where(
        target[:, None, :] == jnp.arange(views * SLAB_DEV)[:, None], all_weight[:, None, :], 0
    ).astype(BF)
    stands = (slot[:, :, None] == jnp.arange(slots)).astype(BF)
    sums = jnp.einsum("gtr,grs->tgs", goes, stands, preferred_element_type=F32)
    sums = sums.astype(BF).reshape(views * SLAB_DEV, owners * slots)
    ramp_part = np.clip((np.arange(KB) + 0.5) / (2.0 * OV), 0.0, 1.0)
    feather = jnp.asarray((np.sin(0.5 * math.pi * ramp_part) ** 2)[None, :], F32)
    return filtered_slabs(got, sums, feather).reshape(views, SLAB_DEV, 2 * channels)


def solution(mesh):
    in_specs = (P("angle", "gz", None), P("angle"), P("angle", "gz"), P("angle", "gz"))
    out_specs = P("angle", "gz", None)
    return jax.shard_map(local, mesh=mesh, in_specs=in_specs, out_specs=out_specs, check_vma=False)
```

```python
import functools
import math

import jax
import jax.numpy as jnp
from jax import lax
from jax.experimental import pallas as pl
from jax.experimental.pallas import tpu as pltpu
from jax.sharding import PartitionSpec as P
import ml_dtypes
import numpy as np

OV = 128
KB = 256
SLAB_DEV = 16
CHUNKS = 4
BF = jnp.bfloat16
F32 = jnp.float32
MESH = pl.DeviceIdType.MESH


def taps(size):
    offset = np.arange(size)[None, :] + size - np.arange(3 * size)[:, None]
    squared = np.maximum(offset.astype(np.float64) ** 2, 1.0)
    values = np.where(
        offset == 0, 0.25, np.where(offset % 2 != 0, -1.0 / (math.pi * math.pi * squared), 0.0)
    )
    return np.where(np.abs(offset) <= size, values, 0.0).astype(np.float32)


def exchange_kernel(
    owners, blocks, chunk, raw_ref, swap_ref, flip_ref, lists_ref, got_ref, got_lists_ref, far,
    flipped, outgoing, near, pick_ref, send_sem, recv_sem, local_sem, far_send, far_recv,
    lists_send, lists_recv, near_send, near_recv,
):
    me_a, me_g = lax.axis_index("angle"), lax.axis_index("gz")
    partner = lax.rem(me_a + blocks // 2, blocks)
    half = owners // 2
    base = me_g // half * half
    place = me_g - base
    far_g = lax.rem(me_g + half, owners)
    slots = outgoing.shape[4]
    parts = raw_ref.shape[1] // chunk
    barrier = pltpu.get_barrier_semaphore()
    for step in range(1, owners):
        pl.semaphore_signal(
            barrier, inc=1, device_id=(me_a, lax.rem(me_g + step, owners)), device_id_type=MESH
        )
    for step in range(half):
        pl.semaphore_signal(
            barrier, inc=1, device_id=(partner, base + lax.rem(place + step, half)),
            device_id_type=MESH,
        )
    pl.semaphore_signal(barrier, inc=1, device_id=(partner, far_g), device_id_type=MESH)
    pl.semaphore_wait(barrier, owners + half)
    nearby = []
    for at, device in enumerate([(me_a, far_g), (partner, me_g), (partner, far_g)]):
        copy = pltpu.make_async_remote_copy(
            src_ref=lists_ref,
            dst_ref=near.at[at],
            send_sem=near_send.at[at],
            recv_sem=near_recv.at[at],
            device_id=device,
            device_id_type=MESH,
        )
        copy.start()
        nearby.append(copy)
    copies, crossing = [], []
    for part in range(parts):
        copy = pltpu.make_async_remote_copy(
            src_ref=raw_ref.at[:, part * chunk:(part + 1) * chunk],
            dst_ref=far.at[part],
            send_sem=far_send.at[part],
            recv_sem=far_recv.at[part],
            device_id=(me_a, far_g),
            device_id_type=MESH,
        )
        copy.start()
        crossing.append(copy)
    for step in range(owners):
        if step == 0:
            copy = pltpu.make_async_copy(lists_ref, got_lists_ref.at[me_g], lists_send.at[0])
        else:
            copy = pltpu.make_async_remote_copy(
                src_ref=lists_ref,
                dst_ref=got_lists_ref.at[me_g],
                send_sem=lists_send.at[step],
                recv_sem=lists_recv.at[step],
                device_id=(me_a, lax.rem(me_g + step, owners)),
                device_id_type=MESH,
            )
        copy.start()
        copies.append(copy)
    rows = raw_ref.shape[0]
    index = lax.broadcasted_iota(jnp.int32, (rows, rows), 0)
    later = jnp.where(index < lax.broadcasted_iota(jnp.int32, (rows, rows), 1), 1.0, 0.0).astype(BF)
    owner_list = lax.broadcasted_iota(jnp.int32, (owners, rows), 0).astype(F32)
    slot_list = lax.broadcasted_iota(jnp.int32, (half * slots, rows), 0) + base * slots
    slot_list = slot_list.astype(F32)

    def picked(owner):
        onehot = jnp.where(owner_list == owner, 1.0, 0.0)
        before = jnp.dot(onehot.astype(BF), later, preferred_element_type=F32)
        slot = owner * slots + jnp.sum(before * onehot, 0, keepdims=True)
        return jnp.where(slot_list == slot, 1.0, 0.0).astype(BF)

    pick_ref[0, 0] = picked(lists_ref[2:3, :rows])
    for copy in nearby:
        copy.wait()
    pick_ref[1, 0] = picked(near[0, 2:3, :rows])
    for origin in range(2):
        mirror = picked(near[1 + origin, 2:3, :rows])
        mirror = jnp.dot(mirror, swap_ref[...], preferred_element_type=F32)
        pick_ref[origin, 1] = mirror.astype(BF)
    width = 2 * KB
    for origin in range(2):
        source_g = me_g if origin == 0 else far_g
        for part in range(parts):
            if origin == 1:
                crossing[part].wait()
            for at in range(chunk // KB):
                begin = part * chunk + at * KB
                block = (
                    raw_ref[:, begin:begin + KB] if origin == 0
                    else far[part, :, at * KB:(at + 1) * KB]
                )
                block = jnp.dot(block, flip_ref[...], preferred_element_type=F32)
                to = chunk - (at + 1) * KB
                flipped[:, to:to + KB] = block.astype(BF)
            for kind in range(2):
                out_part = part if kind == 0 else parts - 1 - part
                for at in range(0, chunk, width):
                    if kind == 1:
                        block = flipped[:, at:at + width]
                    elif origin == 0:
                        block = raw_ref[:, part * chunk + at:part * chunk + at + width]
                    else:
                        block = far[part, :, at:at + width]
                    rows = jnp.dot(pick_ref[origin, kind], block, preferred_element_type=F32)
                    outgoing[out_part, kind, origin, :, :, at:at + width] = (
                        rows.astype(BF).reshape(half, slots, width)
                    )
                target_a = me_a if kind == 0 else partner
                for step in range(half - 1, -1, -1):
                    to = lax.rem(place + step, half)
                    source = outgoing.at[out_part, kind, origin, to]
                    target = got_ref.at[out_part, kind, source_g]
                    if kind == 0 and step == 0:
                        copy = pltpu.make_async_copy(source, target, local_sem.at[part, origin])
                    else:
                        copy = pltpu.make_async_remote_copy(
                            src_ref=source,
                            dst_ref=target,
                            send_sem=send_sem.at[out_part, kind, origin, step],
                            recv_sem=recv_sem.at[out_part, kind, origin, step],
                            device_id=(target_a, base + to),
                            device_id_type=MESH,
                        )
                    copy.start()
                    copies.append(copy)
    for copy in copies:
        copy.wait()


def exchange(raw, swap, flip, lists, owners, blocks, slots):
    rows, channels = raw.shape
    chunk = channels // CHUNKS
    vmem = pl.BlockSpec(memory_space=pltpu.VMEM)
    return pl.pallas_call(
        functools.partial(exchange_kernel, owners, blocks, chunk),
        out_shape=[
            jax.ShapeDtypeStruct((CHUNKS, 2, owners, slots, chunk), BF),
            jax.ShapeDtypeStruct((owners,) + lists.shape, F32),
        ],
        in_specs=[vmem] * 4,
        out_specs=[pl.BlockSpec(memory_space=pl.ANY)] * 2,
        scratch_shapes=[
            pltpu.VMEM((CHUNKS, rows, chunk), BF),
            pltpu.VMEM((rows, chunk), BF),
            pltpu.VMEM((CHUNKS, 2, 2, owners // 2, slots, chunk), BF),
            pltpu.VMEM((3,) + lists.shape, F32),
            pltpu.VMEM((2, 2, owners // 2 * slots, rows), BF),
            pltpu.SemaphoreType.DMA((CHUNKS, 2, 2, owners // 2)),
            pltpu.SemaphoreType.DMA((CHUNKS, 2, 2, owners // 2)),
            pltpu.SemaphoreType.DMA((CHUNKS, 2)),
            pltpu.SemaphoreType.DMA((CHUNKS,)),
            pltpu.SemaphoreType.DMA((CHUNKS,)),
            pltpu.SemaphoreType.DMA((owners,)),
            pltpu.SemaphoreType.DMA((owners,)),
            pltpu.SemaphoreType.DMA((3,)),
            pltpu.SemaphoreType.DMA((3,)),
        ],
        compiler_params=pltpu.CompilerParams(
            collective_id=0, has_side_effects=True, vmem_limit_bytes=48 * 2**20
        ),
        name="exchange",
    )(raw, swap, flip, lists)


def filter_kernel(got_ref, sum_ref, high_ref, low_ref, feather_ref, out_ref, high, low):
    parts, _, _, chunk = got_ref.shape
    channels = parts * chunk
    count = channels // KB
    pad = 2 * KB
    for ref in (high, low):
        ref[:, :pad] = jnp.zeros((ref.shape[0], pad), BF)
        ref[:, ref.shape[1] - pad:] = jnp.zeros((ref.shape[0], pad), BF)

    def summed(kind, at):
        part, begin = at * KB // chunk, at * KB % chunk
        return jnp.dot(
            sum_ref[...], got_ref[part, kind, :, begin:begin + KB], preferred_element_type=F32
        )

    for at in range(2 * count - 1):
        if at < count - 1:
            value = summed(1, at)
        elif at >= count:
            value = summed(0, at - count + 1)
        else:
            weight = feather_ref[...]
            value = weight * summed(0, 0) + (1.0 - weight) * summed(1, at)
        top = value.astype(BF)
        place = pl.ds(pad + at * KB, KB)
        high[:, place] = top
        low[:, place] = (value - top.astype(F32)).astype(BF)
    for at in range(-1, 2 * count):
        window = pl.ds(pad + (at - 1) * KB, 3 * KB)
        value = jnp.dot(high[:, window], high_ref[...], preferred_element_type=F32)
        value += jnp.dot(high[:, window], low_ref[...], preferred_element_type=F32)
        value += jnp.dot(low[:, window], high_ref[...], preferred_element_type=F32)
        value = value.astype(BF)
        begin = OV + at * KB
        if at < 0:
            out_ref[:, :OV] = value[:, OV:]
        elif at == 2 * count - 1:
            out_ref[:, begin:] = value[:, :OV]
        else:
            out_ref[:, begin:begin + KB] = value


def filtered_slabs(got, sums, feather):
    parts, kinds, owners, slots, chunk = got.shape
    channels = parts * chunk
    rows = sums.shape[0]
    tap = taps(KB)
    tap_high = tap.astype(ml_dtypes.bfloat16)
    tap_low = (tap - tap_high.astype(np.float32)).astype(ml_dtypes.bfloat16)
    vmem = pl.BlockSpec(memory_space=pltpu.VMEM)
    return pl.pallas_call(
        filter_kernel,
        out_shape=jax.ShapeDtypeStruct((rows, 2 * channels), BF),
        in_specs=[vmem] * 5,
        out_specs=vmem,
        scratch_shapes=[pltpu.VMEM((rows, 2 * channels - KB + 4 * KB), BF)] * 2,
        compiler_params=pltpu.CompilerParams(vmem_limit_bytes=56 * 2**20),
        name="filter",
    )(got.reshape(parts, kinds, owners * slots, chunk), sums, jnp.asarray(tap_high), jnp.asarray(tap_low), feather)


def ranked(owner, owners):
    rows = owner.shape[-1]
    onehot = (owner[..., None] == jnp.arange(owners)).astype(BF)
    earlier = (jnp.arange(rows)[:, None] > jnp.arange(rows)[None, :]).astype(BF)
    before = jnp.einsum("rk,...ko->...ro", earlier, onehot, preferred_element_type=F32)
    return jnp.sum(before * onehot.astype(F32), -1).astype(jnp.int32)


def local(projections, partner_view, row_weight, row_slab):
    blocks, owners = lax.axis_size("angle"), lax.axis_size("gz")
    views, rows_dev, channels = projections.shape
    rows = views * rows_dev
    capacity = 2 * rows // owners
    slots = -(-capacity // 16) * 16
    lists = jnp.stack([
        row_slab.astype(F32).reshape(rows),
        row_weight.astype(F32).reshape(rows),
        (row_slab // SLAB_DEV).astype(F32).reshape(rows),
    ])
    lists = jnp.pad(lists, ((0, 5), (0, -rows % 128)))
    row = jnp.arange(rows)
    partner_row = jnp.repeat(partner_view % views, rows_dev) * rows_dev + row % rows_dev
    swap = (row[:, None] == partner_row[None, :]).astype(BF)
    flip = (jnp.arange(KB)[:, None] + jnp.arange(KB)[None, :] == KB - 1).astype(BF)
    got, meta = exchange(
        projections.reshape(rows, channels), swap, flip, lists, owners, blocks, slots
    )

    all_slab = meta[:, 0, :rows].astype(jnp.int32)
    all_weight = meta[:, 1, :rows].astype(BF)
    owner = all_slab // SLAB_DEV
    slot = jnp.where(owner == lax.axis_index("gz"), ranked(owner, owners), -1)
    target = jnp.arange(rows) // rows_dev * SLAB_DEV + all_slab % SLAB_DEV
    goes = jnp.where(
        target[:, None, :] == jnp.arange(views * SLAB_DEV)[:, None], all_weight[:, None, :], 0
    ).astype(BF)
    stands = (slot[:, :, None] == jnp.arange(slots)).astype(BF)
    sums = jnp.einsum("gtr,grs->tgs", goes, stands, preferred_element_type=F32)
    sums = sums.astype(BF).reshape(views * SLAB_DEV, owners * slots)
    ramp_part = np.clip((np.arange(KB) + 0.5) / (2.0 * OV), 0.0, 1.0)
    feather = jnp.asarray((np.sin(0.5 * math.pi * ramp_part) ** 2)[None, :], F32)
    return filtered_slabs(got, sums, feather).reshape(views, SLAB_DEV, 2 * channels)


def solution(mesh):
    in_specs = (P("angle", "gz", None), P("angle"), P("angle", "gz"), P("angle", "gz"))
    out_specs = P("angle", "gz", None)
    return jax.shard_map(local, mesh=mesh, in_specs=in_specs, out_specs=out_specs, check_vma=False)
```

```python
import functools
import math

import jax
import jax.numpy as jnp
from jax import lax
from jax.experimental import pallas as pl
from jax.experimental.pallas import tpu as pltpu
from jax.sharding import PartitionSpec as P
import ml_dtypes
import numpy as np

OV = 128
KB = 256
SLAB_DEV = 16
CHUNKS = 4
BF = jnp.bfloat16
F32 = jnp.float32
MESH = pl.DeviceIdType.MESH


def taps(size):
    offset = np.arange(size)[None, :] + size - np.arange(3 * size)[:, None]
    squared = np.maximum(offset.astype(np.float64) ** 2, 1.0)
    values = np.where(
        offset == 0, 0.25, np.where(offset % 2 != 0, -1.0 / (math.pi * math.pi * squared), 0.0)
    )
    return np.where(np.abs(offset) <= size, values, 0.0).astype(np.float32)


def exchange_kernel(
    owners, blocks, chunk, raw_ref, pick_ref, flip_ref, lists_ref, got_ref, got_lists_ref, far,
    flipped, outgoing, send_sem, recv_sem, local_sem, far_send, far_recv, lists_send, lists_recv,
):
    me_a, me_g = lax.axis_index("angle"), lax.axis_index("gz")
    partner = lax.rem(me_a + blocks // 2, blocks)
    half = owners // 2
    base = me_g // half * half
    place = me_g - base
    far_g = lax.rem(me_g + half, owners)
    slots = outgoing.shape[4]
    parts = raw_ref.shape[1] // chunk
    barrier = pltpu.get_barrier_semaphore()
    for step in range(1, owners):
        pl.semaphore_signal(
            barrier, inc=1, device_id=(me_a, lax.rem(me_g + step, owners)), device_id_type=MESH
        )
    for step in range(half):
        pl.semaphore_signal(
            barrier, inc=1, device_id=(partner, base + lax.rem(place + step, half)),
            device_id_type=MESH,
        )
    pl.semaphore_wait(barrier, owners - 1 + half)
    copies, crossing = [], []
    for part in range(parts):
        copy = pltpu.make_async_remote_copy(
            src_ref=raw_ref.at[:, part * chunk:(part + 1) * chunk],
            dst_ref=far.at[part],
            send_sem=far_send.at[part],
            recv_sem=far_recv.at[part],
            device_id=(me_a, far_g),
            device_id_type=MESH,
        )
        copy.start()
        crossing.append(copy)
    for step in range(owners):
        if step == 0:
            copy = pltpu.make_async_copy(lists_ref, got_lists_ref.at[me_g], lists_send.at[0])
        else:
            copy = pltpu.make_async_remote_copy(
                src_ref=lists_ref,
                dst_ref=got_lists_ref.at[me_g],
                send_sem=lists_send.at[step],
                recv_sem=lists_recv.at[step],
                device_id=(me_a, lax.rem(me_g + step, owners)),
                device_id_type=MESH,
            )
        copy.start()
        copies.append(copy)
    width = 2 * KB
    for origin in range(2):
        source_g = me_g if origin == 0 else far_g
        for part in range(parts):
            if origin == 1:
                crossing[part].wait()
            for at in range(chunk // KB):
                begin = part * chunk + at * KB
                block = (
                    raw_ref[:, begin:begin + KB] if origin == 0
                    else far[part, :, at * KB:(at + 1) * KB]
                )
                block = jnp.dot(block, flip_ref[...], preferred_element_type=F32)
                to = chunk - (at + 1) * KB
                flipped[:, to:to + KB] = block.astype(BF)
            for kind in range(2):
                out_part = part if kind == 0 else parts - 1 - part
                for at in range(0, chunk, width):
                    if kind == 1:
                        block = flipped[:, at:at + width]
                    elif origin == 0:
                        block = raw_ref[:, part * chunk + at:part * chunk + at + width]
                    else:
                        block = far[part, :, at:at + width]
                    rows = jnp.dot(pick_ref[origin, kind], block, preferred_element_type=F32)
                    outgoing[out_part, kind, origin, :, :, at:at + width] = (
                        rows.astype(BF).reshape(half, slots, width)
                    )
                target_a = me_a if kind == 0 else partner
                for step in range(half - 1, -1, -1):
                    to = lax.rem(place + step, half)
                    source = outgoing.at[out_part, kind, origin, to]
                    target = got_ref.at[out_part, kind, source_g]
                    if kind == 0 and step == 0:
                        copy = pltpu.make_async_copy(source, target, local_sem.at[part, origin])
                    else:
                        copy = pltpu.make_async_remote_copy(
                            src_ref=source,
                            dst_ref=target,
                            send_sem=send_sem.at[out_part, kind, origin, step],
                            recv_sem=recv_sem.at[out_part, kind, origin, step],
                            device_id=(target_a, base + to),
                            device_id_type=MESH,
                        )
                    copy.start()
                    copies.append(copy)
    for copy in copies:
        copy.wait()


def exchange(raw, pick, flip, lists, owners, blocks, slots):
    rows, channels = raw.shape
    chunk = channels // CHUNKS
    vmem = pl.BlockSpec(memory_space=pltpu.VMEM)
    return pl.pallas_call(
        functools.partial(exchange_kernel, owners, blocks, chunk),
        out_shape=[
            jax.ShapeDtypeStruct((CHUNKS, 2, owners, slots, chunk), BF),
            jax.ShapeDtypeStruct((owners,) + lists.shape, F32),
        ],
        in_specs=[vmem] * 4,
        out_specs=[pl.BlockSpec(memory_space=pl.ANY)] * 2,
        scratch_shapes=[
            pltpu.VMEM((CHUNKS, rows, chunk), BF),
            pltpu.VMEM((rows, chunk), BF),
            pltpu.VMEM((CHUNKS, 2, 2, owners // 2, slots, chunk), BF),
            pltpu.SemaphoreType.DMA((CHUNKS, 2, 2, owners // 2)),
            pltpu.SemaphoreType.DMA((CHUNKS, 2, 2, owners // 2)),
            pltpu.SemaphoreType.DMA((CHUNKS, 2)),
            pltpu.SemaphoreType.DMA((CHUNKS,)),
            pltpu.SemaphoreType.DMA((CHUNKS,)),
            pltpu.SemaphoreType.DMA((owners,)),
            pltpu.SemaphoreType.DMA((owners,)),
        ],
        compiler_params=pltpu.CompilerParams(
            collective_id=0, has_side_effects=True, vmem_limit_bytes=48 * 2**20
        ),
        name="exchange",
    )(raw, pick, flip, lists)


def filter_kernel(got_ref, sum_ref, high_ref, low_ref, feather_ref, out_ref, high, low):
    parts, _, _, chunk = got_ref.shape
    channels = parts * chunk
    count = channels // KB
    pad = 2 * KB
    for ref in (high, low):
        ref[:, :pad] = jnp.zeros((ref.shape[0], pad), BF)
        ref[:, ref.shape[1] - pad:] = jnp.zeros((ref.shape[0], pad), BF)

    def summed(kind, at):
        part, begin = at * KB // chunk, at * KB % chunk
        return jnp.dot(
            sum_ref[...], got_ref[part, kind, :, begin:begin + KB], preferred_element_type=F32
        )

    for at in range(2 * count - 1):
        if at < count - 1:
            value = summed(1, at)
        elif at >= count:
            value = summed(0, at - count + 1)
        else:
            weight = feather_ref[...]
            value = weight * summed(0, 0) + (1.0 - weight) * summed(1, at)
        top = value.astype(BF)
        place = pl.ds(pad + at * KB, KB)
        high[:, place] = top
        low[:, place] = (value - top.astype(F32)).astype(BF)
    for at in range(-1, 2 * count):
        window = pl.ds(pad + (at - 1) * KB, 3 * KB)
        value = jnp.dot(high[:, window], high_ref[...], preferred_element_type=F32)
        value += jnp.dot(high[:, window], low_ref[...], preferred_element_type=F32)
        value += jnp.dot(low[:, window], high_ref[...], preferred_element_type=F32)
        value = value.astype(BF)
        begin = OV + at * KB
        if at < 0:
            out_ref[:, :OV] = value[:, OV:]
        elif at == 2 * count - 1:
            out_ref[:, begin:] = value[:, :OV]
        else:
            out_ref[:, begin:begin + KB] = value


def filtered_slabs(got, sums, feather):
    parts, kinds, owners, slots, chunk = got.shape
    channels = parts * chunk
    rows = sums.shape[0]
    tap = taps(KB)
    tap_high = tap.astype(ml_dtypes.bfloat16)
    tap_low = (tap - tap_high.astype(np.float32)).astype(ml_dtypes.bfloat16)
    vmem = pl.BlockSpec(memory_space=pltpu.VMEM)
    return pl.pallas_call(
        filter_kernel,
        out_shape=jax.ShapeDtypeStruct((rows, 2 * channels), BF),
        in_specs=[vmem] * 5,
        out_specs=vmem,
        scratch_shapes=[pltpu.VMEM((rows, 2 * channels - KB + 4 * KB), BF)] * 2,
        compiler_params=pltpu.CompilerParams(vmem_limit_bytes=56 * 2**20),
        name="filter",
    )(got.reshape(parts, kinds, owners * slots, chunk), sums, jnp.asarray(tap_high), jnp.asarray(tap_low), feather)


def ranked(owner, owners):
    rows = owner.shape[-1]
    onehot = (owner[..., None] == jnp.arange(owners)).astype(BF)
    earlier = (jnp.arange(rows)[:, None] > jnp.arange(rows)[None, :]).astype(BF)
    before = jnp.einsum("rk,...ko->...ro", earlier, onehot, preferred_element_type=F32)
    return jnp.sum(before * onehot.astype(F32), -1).astype(jnp.int32)


def local(projections, partner_view, row_weight, row_slab):
    blocks, owners = lax.axis_size("angle"), lax.axis_size("gz")
    views, rows_dev, channels = projections.shape
    rows = views * rows_dev
    capacity = 2 * rows // owners
    slots = -(-capacity // 16) * 16
    half = blocks // 2
    other_slab = lax.ppermute(row_slab, "angle", [(s, (s + half) % blocks) for s in range(blocks)])
    lists = jnp.concatenate([row_slab.astype(F32), row_weight.astype(F32)], 0)
    lists = jnp.pad(lists, ((0, 0), (0, 128 - rows_dev)))

    def slot_of(slab):
        owner = slab.reshape(rows) // SLAB_DEV
        return owner * slots + ranked(owner, owners)

    pair = jnp.stack([row_slab, other_slab])
    far = owners // 2
    shift = [(s, (s + far) % owners) for s in range(owners)]
    both = [
        (s * owners + t, (s + half) % blocks * owners + (t + far) % owners)
        for s in range(blocks) for t in range(owners)
    ]
    far_pair = [
        lax.ppermute(row_slab, "gz", shift), lax.ppermute(row_slab, ("angle", "gz"), both)
    ]
    local_partner = partner_view % views
    is_partner = (local_partner[:, None] == jnp.arange(views)[None, :]).astype(jnp.int32)
    slot_list = (lax.axis_index("gz") // far * far * slots + jnp.arange(far * slots))[:, None]

    def picks(own_slab, partner_slab):
        own_slot = slot_of(own_slab)
        other_slot = slot_of(partner_slab).reshape(views, rows_dev)
        mirror_slot = jnp.sum(is_partner[:, :, None] * other_slot[None], 1).reshape(rows)
        return jnp.stack([own_slot[None, :] == slot_list, mirror_slot[None, :] == slot_list])

    pick = jnp.stack([picks(pair[0], pair[1]), picks(far_pair[0], far_pair[1])]).astype(BF)
    flip = (jnp.arange(KB)[:, None] + jnp.arange(KB)[None, :] == KB - 1).astype(BF)
    got, meta = exchange(
        projections.reshape(rows, channels), pick, flip, lists, owners, blocks, slots
    )
    meta = meta[:, :, :rows_dev]

    all_slab = meta[:, :views].reshape(owners, rows).astype(jnp.int32)
    all_weight = meta[:, views:].reshape(owners, rows).astype(BF)
    owner = all_slab // SLAB_DEV
    slot = jnp.where(owner == lax.axis_index("gz"), ranked(owner, owners), -1)
    target = jnp.arange(rows) // rows_dev * SLAB_DEV + all_slab % SLAB_DEV
    goes = jnp.where(
        target[:, None, :] == jnp.arange(views * SLAB_DEV)[:, None], all_weight[:, None, :], 0
    ).astype(BF)
    stands = (slot[:, :, None] == jnp.arange(slots)).astype(BF)
    sums = jnp.einsum("gtr,grs->tgs", goes, stands, preferred_element_type=F32)
    sums = sums.astype(BF).reshape(views * SLAB_DEV, owners * slots)
    ramp_part = np.clip((np.arange(KB) + 0.5) / (2.0 * OV), 0.0, 1.0)
    feather = jnp.asarray((np.sin(0.5 * math.pi * ramp_part) ** 2)[None, :], F32)
    return filtered_slabs(got, sums, feather).reshape(views, SLAB_DEV, 2 * channels)


def solution(mesh):
    in_specs = (P("angle", "gz", None), P("angle"), P("angle", "gz"), P("angle", "gz"))
    out_specs = P("angle", "gz", None)
    return jax.shard_map(local, mesh=mesh, in_specs=in_specs, out_specs=out_specs, check_vma=False)
```
